128 devices in a mesh: row: 8 (over y, core), col: 16 (over z, x).
Axes of the slice: x: 4, y: 4, z: 4, core: 2. Of those that a mesh axis runs over, the one named last changes fastest.
Arguments:
- volts: bfloat16 [2, 512, 16384], P(None, ('row', 'col')), may hold values from -6 to 6
- pattern: int32 [128, 128], replicated, may hold values from -1 to 254, as said below
- owner_slot: int32 [256], replicated, may hold values from 0 to 255, each once
Outputs:
- stacks: float32 [256, 4, 255], P(('row', 'col'))
The draws below stay inside these ranges and needn't reach their ends.
Inputs may be any that keep to these rules, and one draw needn't show every extreme that they name: pattern[p, q] is either q - p + 127 or -1; it is -1 where p == q. `owner_slot`: a permutation.
All inputs are finite; a program needn't handle non-finite values.
Results may differ from the reference program's by a relative error of at most 0.0003.
Values may be sent and summed in bfloat16 or wider, within the bound.
No kernel may reach another device: no remote copies, remote signals or barrier semaphores. Data moves between devices by JAX's collectives and lax.ppermute only.
A program may use at most 64 MiB of HBM per device.

```python
import jax
import jax.numpy as jnp
from jax import lax

GRID_COLUMNS = 128
CHAN = 2
TIME_SAMPLES = 256
GR = 128
ANTENNA_COUNT = 16384
CHANNEL_SAMPLES = 512
NSTACK = 256
KSEP = 255


def draw_pattern(key, part):
    key = jax.random.fold_in(key, 7)
    first = jnp.arange(GR, dtype=jnp.int32)[:, None]
    second = jnp.arange(GR, dtype=jnp.int32)[None, :]
    flagged = jax.random.randint(key, (GR, GR), 0, 8) == 0
    corner = (first == 0) & (second == GR - 1)
    keep = (jnp.logical_not(flagged) | corner) & (first != second)
    return jnp.where(keep, second - first + GR - 1, -1).astype(jnp.int32)


def steps_of(key, extent, shards, least, top_value):
    gain = 1.0
    for position, blocks in shards:
        steps = jax.random.uniform(jax.random.fold_in(jax.random.fold_in(key, 6), position), (blocks,), jnp.float32, least / len(shards), top_value / len(shards))
        gain = gain * jnp.repeat(jnp.exp(steps), extent[position] // blocks).reshape((-1,) + (1,) * (len(extent) - 1 - position))
    return gain


def centred(key, extent, deviation, limit, split=(), kind=jnp.bfloat16):
    result = jax.random.normal(key, extent, jnp.float32) * deviation
    if len(split) > 0:
        result = steps_of(key, extent, split, -0.22, 0.18) * result
    return jnp.clip(result, min=-limit, max=limit).astype(kind)


def setup_inputs(seed: int = 0) -> dict:
    key_of = jax.random.split(jax.random.key(seed), 4)
    return {
        "volts": centred(key_of[0], (2, CHANNEL_SAMPLES, ANTENNA_COUNT), 1.0, 6.0, ((1, 128),)),
        "pattern": draw_pattern(jax.random.fold_in(key_of[3], 71), 0),
        "owner_slot": jax.random.permutation(key_of[2], NSTACK).astype(jnp.int32),
    }


def fold_diagonals(blocks):
    width = blocks.shape[-1]
    lead = blocks.shape[:-2]
    flipped = blocks[..., ::-1, :]
    padded = jnp.pad(flipped, [(0, 0)] * (blocks.ndim - 1) + [(0, width)])
    flat = padded.reshape(lead + (2 * width * width,))[..., :width * (2 * width - 1)]
    return flat.reshape(lead + (width, 2 * width - 1)).sum(axis=-2)

def reference(volts, pattern, owner_slot):
    voltages = volts.astype(jnp.float32).reshape(2, CHAN, TIME_SAMPLES, GR, GRID_COLUMNS)
    rotated = jnp.stack([-voltages[1], voltages[0]])
    highest = lax.Precision.HIGHEST

    def row_step(totals, grid_row):
        current = lax.dynamic_index_in_dim(voltages, grid_row, 3, keepdims=False)
        real_part = jnp.einsum('xcta,xctqb->cqab', current, voltages, precision=highest)
        imag_part = jnp.einsum('xcta,xctqb->cqab', current, rotated, precision=highest)
        folded = fold_diagonals(jnp.stack([real_part, imag_part], axis=1))
        folded = folded.transpose(2, 0, 1, 3).reshape(GR, 2 * CHAN, KSEP)
        keys = lax.dynamic_index_in_dim(pattern, grid_row, 0, keepdims=False)
        segment = jnp.where(keys >= 0, keys, NSTACK).astype(jnp.int32)
        summed = jax.ops.segment_sum(folded, segment, NSTACK + 1)[:NSTACK]
        return (totals + summed, None)
    start = jnp.zeros((NSTACK, 2 * CHAN, KSEP), jnp.float32)
    totals, unused = lax.scan(row_step, start, jnp.arange(GR, dtype=jnp.int32))
    flat_keys = pattern.reshape(-1)
    segment = jnp.where(flat_keys >= 0, flat_keys, NSTACK).astype(jnp.int32)
    pair_counts = jax.ops.segment_sum(jnp.ones(flat_keys.shape, jnp.float32), segment, NSTACK + 1)[:NSTACK]
    separation_offsets = jnp.abs(jnp.arange(KSEP, dtype=jnp.float32) - (GRID_COLUMNS - 1.0))
    antenna_pairs = pair_counts[:, None] * (GRID_COLUMNS - separation_offsets)[None, :]
    stack_scale = 1.0 / jnp.sqrt(2.0 * TIME_SAMPLES * jnp.maximum(antenna_pairs, 1.0))
    normed = totals * stack_scale[:, None, :]
    return jnp.zeros_like(normed).at[owner_slot].set(normed)
```

```python
import jax
import jax.numpy as jnp
import numpy as np
from jax import lax
from jax.experimental import pallas as pl
from jax.experimental.pallas import tpu as pltpu
from jax.sharding import PartitionSpec as P

GRID_COLUMNS = 128
CHAN = 2
TIME_SAMPLES = 256
BINS = 2 * GRID_COLUMNS
HALF = BINS // 2
F32 = jnp.float32
BF16 = jnp.bfloat16


def split_table(table):
    table = table.astype(np.float32)
    high = table.astype(jnp.bfloat16)
    low = (table - high.astype(np.float32)).astype(jnp.bfloat16)
    return np.stack([high, low])


def forward_table():
    angle = 2.0 * np.pi * np.outer(np.arange(HALF), np.arange(GRID_COLUMNS)) / BINS
    cosine, sine = np.cos(angle), np.sin(angle)
    return split_table(np.block([[cosine, sine], [-sine, cosine]]))


def inverse_table():
    lag = np.arange(BINS) - (GRID_COLUMNS - 1)
    angle = 2.0 * np.pi * np.outer(np.arange(HALF), lag) / BINS
    return split_table(np.concatenate([np.cos(angle), np.sin(angle)]) / BINS)


def dot(left, right, contract):
    return lax.dot_general(left, right, ((contract[:1], contract[1:]), ((), ())), preferred_element_type=F32)


def halves(value):
    high = value.astype(BF16)
    return high, (value - high.astype(F32)).astype(BF16)


def skew(value):
    return pltpu.roll(value, 1, 1, stride=1, stride_axis=0)


def stack_kernel(core_ref, own_ref, peer_ref, table_ref, pattern_ref, slots_ref, out_ref, rows_ref, bins_ref, mask_ref, sums_ref):
    width = GRID_COLUMNS
    lane = lax.broadcasted_iota(jnp.int32, (1, width), 1)
    sign = jnp.where((lane % 2 == 1) & (core_ref[0] == 1), -1.0, 1.0).astype(F32)
    for part in range(2):
        for place, source in ((0, own_ref), (4, peer_ref)):
            for grid_row in range(width):
                piece = source[part, :, grid_row * width:(grid_row + 1) * width].astype(F32)
                rows_ref[part, grid_row * 8 + place:grid_row * 8 + place + 4, :] = piece * sign
    for sample in range(8):
        volts = jnp.concatenate(
            [rows_ref[part, pl.ds(sample, width, stride=8), :].astype(BF16) for part in range(2)], axis=1
        )
        bins = dot(table_ref[0], volts, (1, 1)) + dot(table_ref[1], volts, (1, 1))
        bins_ref[pl.ds(sample, HALF, stride=16), :] = bins[:HALF]
        bins_ref[pl.ds(sample + 8, HALF, stride=16), :] = bins[HALF:]
    row = lax.broadcasted_iota(jnp.int32, (width, width), 0)
    column = lax.broadcasted_iota(jnp.int32, (width, width), 1)
    reverse = (row + column == width - 1).astype(F32).astype(BF16)
    valid = (pattern_ref[...] >= 0).astype(F32).astype(BF16)
    upper = column <= row
    for which in range(2):
        mask = skew(dot(reverse, valid, (1, which)))
        mask_ref[2 * which] = jnp.where(upper, mask, 0.0)
        mask_ref[2 * which + 1] = jnp.where(upper, 0.0, mask)

    def some_bins(step, carry):
        lines = []
        for pair in range(4):
            lefts, rights = [], []
            for inner in range(2):
                left = bins_ref[pl.ds(step * 128 + pair * 32 + inner * 16, 16), :]
                real, imag = left[:8], left[8:]
                right = jnp.concatenate([real - imag, real + imag], axis=0)
                left_high, left_low = halves(left)
                right_high, right_low = halves(right)
                lefts += [left_high, left_high, left_low]
                right = jnp.concatenate([right_high, right_low, right_high], axis=0)
                empty = jnp.zeros_like(right)
                rights.append(jnp.concatenate([empty, right] if inner else [right, empty], axis=1))
            turned = dot(reverse, jnp.concatenate(lefts, axis=0), (1, 1)).astype(BF16)
            both = dot(turned, jnp.concatenate(rights, axis=0), (1, 0))
            for inner in range(2):
                product = skew(both[:, inner * width:(inner + 1) * width])
                line = []
                for which in range(4):
                    total = None
                    for tile in range(16):
                        span = slice(tile * 8, tile * 8 + 8)
                        term = product[span] * mask_ref[which, span, :]
                        total = term if total is None else total + term
                    line.append(jnp.sum(total, axis=0, keepdims=True))
                lines.append(jnp.concatenate(line, axis=1))
        sums_ref[pl.ds(pl.multiple_of(step * 8, 8), 8), :] = jnp.concatenate(lines, axis=0)
        return carry

    lax.fori_loop(0, HALF // 8, some_bins, 0)
    index = lax.broadcasted_iota(jnp.int32, (4 * width, 4 * width), 0)
    slot = 2 * (index // 4) + (index // 2) % 2
    mirrored = lax.broadcasted_iota(jnp.int32, (4 * width, 4 * width), 1) >= 2 * width
    weight = jnp.where(mirrored & (index % 2 == 1), -0.5, 0.5)
    place = jnp.where(slots_ref[...] == slot, weight, 0.0).astype(BF16)
    sums_high, sums_low = halves(sums_ref[...])
    out_ref[...] = dot(place, sums_high, (1, 1)) + dot(place, sums_low, (1, 1))


def owner_kernel(device_ref, parts_ref, table_ref, pattern_ref, slots_ref, out_ref):
    device = device_ref[0]
    lane = lax.broadcasted_iota(jnp.int32, (1, BINS), 1)
    lag = lane - (GRID_COLUMNS - 1)
    lines = []
    for core in range(2):
        for chan in range(CHAN):
            total = None
            for near in range(2):
                first = ((chan * 2 + near) * 2 + core) * 16
                part = jnp.sum(parts_ref[first:first + 16], axis=0)
                total = part if total is None else total + part
            for slot in range(2):
                real, imag = total[2 * slot:2 * slot + 1], total[2 * slot + 1:2 * slot + 2]
                lines.append(jnp.concatenate([real, imag], axis=1))
                lines.append(jnp.concatenate([imag, -real], axis=1))
    high, low = halves(jnp.concatenate(lines, axis=0))
    turned = dot(high, table_ref[0], (1, 0)) + dot(low, table_ref[0], (1, 0)) + dot(high, table_ref[1], (1, 0))
    turned = turned[:8] + jnp.where(lane % 2 == 1, 1.0, -1.0) * turned[8:]
    reach = GRID_COLUMNS - jnp.abs(lag).astype(F32)
    stack = lax.broadcasted_iota(jnp.int32, (1, BINS), 1)
    for slot in range(2):
        key = jnp.sum(jnp.where(slots_ref[...] == 2 * device + slot, stack, 0), axis=1, keepdims=True)
        count = jnp.sum((pattern_ref[...] == key).astype(F32), axis=(0, 1), keepdims=True)
        scale = 1.0 / jnp.sqrt(2.0 * TIME_SAMPLES * jnp.maximum(count * reach, 1.0))
        for chan in range(CHAN):
            for part in range(2):
                line = chan * 4 + slot * 2 + part
                value = turned[line:line + 1] * scale
                out_ref[slot, 2 * chan + part:2 * chan + part + 1, :] = value[:, :BINS - 1]


def per_device(volts, pattern, owner_slot):
    width = GRID_COLUMNS
    row_index = lax.axis_index("row")
    core = (row_index % 2).reshape(1)
    device = lax.axis_index(("row", "col")).reshape(1)
    row_count = lax.axis_size("row")
    swap = [(i, i ^ 1) for i in range(row_count)]
    peer = lax.ppermute(volts, "row", swap)
    none = jnp.full((1,), -1, jnp.int32)
    low_slots, high_slots = owner_slot[:width], owner_slot[width:]
    slots = jnp.concatenate([
        none, high_slots[:width - 1],
        none, low_slots[:width - 1],
        none, low_slots[:width - 1][::-1],
        none, high_slots[:width - 1][::-1],
    ])[None]
    vmem = pl.BlockSpec(memory_space=pltpu.VMEM)
    smem = pl.BlockSpec(memory_space=pltpu.SMEM)
    partial = pl.pallas_call(
        stack_kernel,
        out_shape=jax.ShapeDtypeStruct((4 * width, HALF), F32),
        in_specs=[smem, vmem, vmem, vmem, vmem, vmem],
        out_specs=vmem,
        scratch_shapes=[
            pltpu.VMEM((2, 8 * width, width), F32),
            pltpu.VMEM((16 * HALF, width), F32),
            pltpu.VMEM((4, width, width), F32),
            pltpu.VMEM((HALF, 4 * width), F32),
        ],
        compiler_params=pltpu.CompilerParams(vmem_limit_bytes=48 * 2 ** 20),
        name="stack_kernel",
    )(core, volts, peer, jnp.asarray(forward_table()), pattern, slots)
    parts = lax.all_to_all(partial.reshape(width, 4, HALF), ("row", "col"), split_axis=0, concat_axis=0, tiled=True)
    return pl.pallas_call(
        owner_kernel,
        out_shape=jax.ShapeDtypeStruct((2, 2 * CHAN, BINS - 1), F32),
        in_specs=[smem, vmem, vmem, vmem, vmem],
        out_specs=vmem,
        compiler_params=pltpu.CompilerParams(vmem_limit_bytes=48 * 2 ** 20),
        name="owner_kernel",
    )(device, parts, jnp.asarray(inverse_table()), pattern, owner_slot[None])


def solution(mesh):
    return jax.shard_map(
        per_device,
        mesh=mesh,
        in_specs=(P(None, ("row", "col"), None), P(), P()),
        out_specs=P(("row", "col"), None, None),
        check_vma=False,
    )
```

```python
import jax
import jax.numpy as jnp
import numpy as np
from jax import lax
from jax.experimental import pallas as pl
from jax.experimental.pallas import tpu as pltpu
from jax.sharding import PartitionSpec as P

GRID_COLUMNS = 128
CHAN = 2
TIME_SAMPLES = 256
BINS = 2 * GRID_COLUMNS
HALF = BINS // 2
F32 = jnp.float32
BF16 = jnp.bfloat16


def split_table(table):
    table = table.astype(np.float32)
    high = table.astype(jnp.bfloat16)
    low = (table - high.astype(np.float32)).astype(jnp.bfloat16)
    return np.stack([high, low])


def forward_table():
    angle = 2.0 * np.pi * np.outer(np.arange(HALF), np.arange(GRID_COLUMNS)) / BINS
    cosine, sine = np.cos(angle), np.sin(angle)
    return split_table(np.block([[cosine, sine], [-sine, cosine]]))


def inverse_table():
    lag = np.arange(BINS) - (GRID_COLUMNS - 1)
    angle = 2.0 * np.pi * np.outer(np.arange(HALF), lag) / BINS
    return split_table(np.concatenate([np.cos(angle), np.sin(angle)]) / BINS)


def dot(left, right, contract):
    return lax.dot_general(left, right, ((contract[:1], contract[1:]), ((), ())), preferred_element_type=F32)


def halves(value):
    high = value.astype(BF16)
    return high, (value - high.astype(F32)).astype(BF16)


def skew(value):
    return pltpu.roll(value, 1, 1, stride=1, stride_axis=0)


def spread(source, rows_ref, core):
    lane = lax.broadcasted_iota(jnp.int32, (1, GRID_COLUMNS), 1)
    sign = jnp.where((lane % 2 == 1) & (core == 1), -1.0, 1.0).astype(F32)
    for part in range(2):
        for grid_row in range(GRID_COLUMNS):
            piece = source[part, :, grid_row * GRID_COLUMNS:(grid_row + 1) * GRID_COLUMNS].astype(F32)
            rows_ref[part, grid_row * 4:grid_row * 4 + 4, :] = piece * sign


def transform(rows_ref, table_ref, bins_ref):
    for sample in range(4):
        volts = jnp.concatenate(
            [rows_ref[part, pl.ds(sample, GRID_COLUMNS, stride=4), :].astype(BF16) for part in range(2)], axis=1
        )
        bins = dot(table_ref[0], volts, (1, 1)) + dot(table_ref[1], volts, (1, 1))
        bins_ref[pl.ds(sample, HALF, stride=8), :] = bins[:HALF]
        bins_ref[pl.ds(sample + 4, HALF, stride=8), :] = bins[HALF:]


def reversal():
    row = lax.broadcasted_iota(jnp.int32, (GRID_COLUMNS, GRID_COLUMNS), 0)
    column = lax.broadcasted_iota(jnp.int32, (GRID_COLUMNS, GRID_COLUMNS), 1)
    return (row + column == GRID_COLUMNS - 1).astype(F32).astype(BF16)


def own_kernel(core_ref, own_hbm, table_hbm, pattern_hbm, slots_hbm, bins_ref, mask_ref, place_ref, table_ref,
               own_ref, pattern_ref, slots_ref, rows_ref, own_sem, table_sem, pattern_sem, slots_sem):
    width = GRID_COLUMNS
    slots_copy = pltpu.make_async_copy(slots_hbm, slots_ref, slots_sem)
    own_copy = pltpu.make_async_copy(own_hbm, own_ref, own_sem)
    table_copy = pltpu.make_async_copy(table_hbm, table_ref, table_sem)
    pattern_copy = pltpu.make_async_copy(pattern_hbm, pattern_ref, pattern_sem)
    slots_copy.start()
    own_copy.start()
    pattern_copy.start()
    table_copy.start()
    reverse = reversal()
    slots_copy.wait()
    order = slots_ref[...].astype(F32)
    low, high = order[:, :width], order[:, width:]
    ahead = [pltpu.roll(half, 1, 1) for half in (high, low)]
    behind = [dot(half.astype(BF16), reverse, (1, 0)) for half in (low, high)]
    first = lax.broadcasted_iota(jnp.int32, (1, width), 1) == 0
    lane_slot = jnp.concatenate([jnp.where(first, -1.0, half) for half in ahead + behind], axis=1).astype(jnp.int32)
    index = lax.broadcasted_iota(jnp.int32, (4 * width, 4 * width), 0)
    slot = 2 * (index // 4) + (index // 2) % 2
    mirrored = lax.broadcasted_iota(jnp.int32, (4 * width, 4 * width), 1) >= 2 * width
    weight = jnp.where(mirrored & (index % 2 == 1), -0.5, 0.5)
    place_ref[...] = jnp.where(lane_slot == slot, weight, 0.0).astype(BF16)
    own_copy.wait()
    spread(own_ref, rows_ref, core_ref[0])
    pattern_copy.wait()
    valid = (pattern_ref[...] >= 0).astype(F32).astype(BF16)
    row = lax.broadcasted_iota(jnp.int32, (width, width), 0)
    column = lax.broadcasted_iota(jnp.int32, (width, width), 1)
    for which in range(2):
        mask = skew(dot(reverse, valid, (1, which)))
        mask_ref[2 * which] = jnp.where(column <= row, mask, 0.0)
        mask_ref[2 * which + 1] = jnp.where(column <= row, 0.0, mask)
    table_copy.wait()
    transform(rows_ref, table_ref, bins_ref)


def stack_kernel(core_ref, peer_ref, own_bins_ref, mask_ref, place_ref, table_ref, out_ref,
                 rows_ref, peer_bins_ref, sums_ref, left_ref, right_ref, gram_ref):
    width = GRID_COLUMNS
    spread(peer_ref, rows_ref, core_ref[0])
    transform(rows_ref, table_ref, peer_bins_ref)
    reverse = reversal()
    minus = jnp.where(lax.broadcasted_iota(jnp.int32, (8, width), 0) < 4, -1.0, 1.0).astype(F32)

    def turn_bins(step):
        lefts = []
        for inner in range(8):
            first = step * 64 + inner * 8
            left, right = [], []
            for source in (own_bins_ref, peer_bins_ref):
                tile = source[first:first + 8, :]
                left.append(tile)
                right.append(tile + minus * pltpu.roll(tile, 4, 0))
            left_high, left_low = halves(jnp.concatenate(left, axis=0))
            right_high, right_low = halves(jnp.concatenate(right, axis=0))
            lefts += [left_high, left_high, left_low, left_low]
            right_ref[step * 8 + inner] = jnp.concatenate([right_high, right_low, right_high, right_low], axis=0)
        left_ref[step] = dot(reverse, jnp.concatenate(lefts, axis=0), (1, 1)).astype(BF16)

    def gram_bins(step):
        for pair in range(4):
            rights = []
            for inner in range(2):
                right = right_ref[step * 8 + pair * 2 + inner]
                empty = jnp.zeros_like(right)
                rights.append(jnp.concatenate([empty, right] if inner else [right, empty], axis=1))
            left = left_ref[step, :, pair * width:(pair + 1) * width]
            gram_ref[step * 4 + pair] = dot(left, jnp.concatenate(rights, axis=0), (1, 0))

    def sum_bins(step):
        lines = []
        for quad in range(2):
            totals = [[None] * 4 for bin in range(4)]
            for tile in range(16):
                span = slice(tile * 8, tile * 8 + 8)
                masks = [mask_ref[which, span, :] for which in range(4)]
                for bin in range(4):
                    place = step * 4 + quad * 2 + bin // 2
                    lanes = slice(bin % 2 * width, bin % 2 * width + width)
                    shift = (1 + 8 * tile) % width
                    product = pltpu.roll(gram_ref[place, span, lanes], shift, 1, stride=1, stride_axis=0)
                    for which in range(4):
                        term = product * masks[which]
                        totals[bin][which] = term if tile == 0 else totals[bin][which] + term
            for bin in range(4):
                lines.append(jnp.concatenate([jnp.sum(total, axis=0, keepdims=True) for total in totals[bin]], axis=1))
        sums_ref[step * 8:step * 8 + 8, :] = jnp.concatenate(lines, axis=0)

    steps = HALF // 8
    for step in range(steps + 2):
        if step < steps:
            turn_bins(step)
        if 1 <= step <= steps:
            gram_bins(step - 1)
        if 2 <= step:
            sum_bins(step - 2)
    sums_high, sums_low = halves(sums_ref[...])
    out_ref[...] = dot(place_ref[...], sums_high, (1, 1)) + dot(place_ref[...], sums_low, (1, 1))


def owner_kernel(device_ref, parts_ref, table_ref, pattern_ref, slots_ref, out_ref):
    device = device_ref[0]
    lane = lax.broadcasted_iota(jnp.int32, (1, BINS), 1)
    lag = lane - (GRID_COLUMNS - 1)
    lines = []
    for core in range(2):
        for chan in range(CHAN):
            total = None
            for near in range(2):
                first = ((chan * 2 + near) * 2 + core) * 16
                part = jnp.sum(parts_ref[first:first + 16], axis=0)
                total = part if total is None else total + part
            for slot in range(2):
                real, imag = total[2 * slot:2 * slot + 1], total[2 * slot + 1:2 * slot + 2]
                lines.append(jnp.concatenate([real, imag], axis=1))
                lines.append(jnp.concatenate([imag, -real], axis=1))
    high, low = halves(jnp.concatenate(lines, axis=0))
    turned = dot(high, table_ref[0], (1, 0)) + dot(low, table_ref[0], (1, 0)) + dot(high, table_ref[1], (1, 0))
    turned = turned[:8] + jnp.where(lane % 2 == 1, 1.0, -1.0) * turned[8:]
    reach = GRID_COLUMNS - jnp.abs(lag).astype(F32)
    stack = lax.broadcasted_iota(jnp.int32, (1, BINS), 1)
    for slot in range(2):
        key = jnp.sum(jnp.where(slots_ref[...] == 2 * device + slot, stack, 0), axis=1, keepdims=True)
        count = jnp.sum((pattern_ref[...] == key).astype(F32), axis=(0, 1), keepdims=True)
        scale = 1.0 / jnp.sqrt(2.0 * TIME_SAMPLES * jnp.maximum(count * reach, 1.0))
        for chan in range(CHAN):
            for part in range(2):
                line = chan * 4 + slot * 2 + part
                value = turned[line:line + 1] * scale
                out_ref[slot, 2 * chan + part:2 * chan + part + 1, :] = value[:, :BINS - 1]


def per_device(volts, pattern, owner_slot):
    width = GRID_COLUMNS
    row_index = lax.axis_index("row")
    core = (row_index % 2).reshape(1)
    device = lax.axis_index(("row", "col")).reshape(1)
    row_count = lax.axis_size("row")
    swap = [(i, i ^ 1) for i in range(row_count)]
    peer = lax.ppermute(volts, "row", swap)
    vmem = pl.BlockSpec(memory_space=pltpu.VMEM)
    smem = pl.BlockSpec(memory_space=pltpu.SMEM)
    anywhere = pl.BlockSpec(memory_space=pltpu.HBM)
    prepared = pl.pallas_call(
        own_kernel,
        out_shape=[
            jax.ShapeDtypeStruct((8 * HALF, width), F32),
            jax.ShapeDtypeStruct((4, width, width), F32),
            jax.ShapeDtypeStruct((4 * width, 4 * width), BF16),
            jax.ShapeDtypeStruct((2, BINS, BINS), BF16),
        ],
        in_specs=[smem] + [anywhere] * 4,
        out_specs=[vmem] * 4,
        scratch_shapes=[
            pltpu.VMEM(volts.shape, BF16),
            pltpu.VMEM(pattern.shape, jnp.int32),
            pltpu.VMEM((1, 2 * width), jnp.int32),
            pltpu.VMEM((2, 4 * width, width), F32),
            pltpu.SemaphoreType.DMA,
            pltpu.SemaphoreType.DMA,
            pltpu.SemaphoreType.DMA,
            pltpu.SemaphoreType.DMA,
        ],
        compiler_params=pltpu.CompilerParams(vmem_limit_bytes=16 * 2 ** 20),
        name="own_kernel",
    )(core, *[pltpu.with_memory_space_constraint(x, pltpu.HBM) for x in (volts, jnp.asarray(forward_table()), pattern, owner_slot[None])])
    partial = pl.pallas_call(
        stack_kernel,
        out_shape=jax.ShapeDtypeStruct((4 * width, HALF), F32),
        in_specs=[smem] + [vmem] * 5,
        out_specs=vmem,
        scratch_shapes=[
            pltpu.VMEM((2, 4 * width, width), F32),
            pltpu.VMEM((8 * HALF, width), F32),
            pltpu.VMEM((HALF, 4 * width), F32),
            pltpu.VMEM((HALF // 8, width, 4 * width), BF16),
            pltpu.VMEM((HALF, 64, width), BF16),
            pltpu.VMEM((HALF // 2, width, 2 * width), F32),
        ],
        compiler_params=pltpu.CompilerParams(vmem_limit_bytes=32 * 2 ** 20),
        name="stack_kernel",
    )(core, peer, *prepared)
    parts = lax.all_to_all(partial.reshape(width, 4, HALF), ("row", "col"), split_axis=0, concat_axis=0, tiled=True)
    return pl.pallas_call(
        owner_kernel,
        out_shape=jax.ShapeDtypeStruct((2, 2 * CHAN, BINS - 1), F32),
        in_specs=[smem, vmem, vmem, vmem, vmem],
        out_specs=vmem,
        compiler_params=pltpu.CompilerParams(vmem_limit_bytes=16 * 2 ** 20),
        name="owner_kernel",
    )(device, parts, jnp.asarray(inverse_table()), pattern, owner_slot[None])


def solution(mesh):
    return jax.shard_map(
        per_device,
        mesh=mesh,
        in_specs=(P(None, ("row", "col"), None), P(), P()),
        out_specs=P(("row", "col"), None, None),
        check_vma=False,
    )
```

```python
import jax
import jax.numpy as jnp
import numpy as np
from jax import lax
from jax.experimental import pallas as pl
from jax.experimental.pallas import tpu as pltpu
from jax.sharding import PartitionSpec as P

GRID_COLUMNS = 128
CHAN = 2
TIME_SAMPLES = 256
BINS = 2 * GRID_COLUMNS
HALF = BINS // 2
F32 = jnp.float32
BF16 = jnp.bfloat16


def split_table(table):
    table = table.astype(np.float32)
    high = table.astype(jnp.bfloat16)
    low = (table - high.astype(np.float32)).astype(jnp.bfloat16)
    return np.stack([high, low])


def forward_table():
    angle = 2.0 * np.pi * np.outer(np.arange(HALF), np.arange(GRID_COLUMNS)) / BINS
    cosine, sine = np.cos(angle), np.sin(angle)
    return split_table(np.block([[cosine, sine], [-sine, cosine]]))


def inverse_table():
    lag = np.arange(BINS) - (GRID_COLUMNS - 1)
    angle = 2.0 * np.pi * np.outer(np.arange(HALF), lag) / BINS
    return split_table(np.concatenate([np.cos(angle), np.sin(angle)]) / BINS)


def dot(left, right, contract):
    return lax.dot_general(left, right, ((contract[:1], contract[1:]), ((), ())), preferred_element_type=F32)


def halves(value):
    high = value.astype(BF16)
    return high, (value - high.astype(F32)).astype(BF16)


def skew(value):
    return pltpu.roll(value, 1, 1, stride=1, stride_axis=0)


BATCH = 2


def spread(source, rows_ref, core):
    lane = lax.broadcasted_iota(jnp.int32, (1, GRID_COLUMNS), 1)
    sign = jnp.where((lane % 2 == 1) & (core == 1), -1.0, 1.0).astype(F32)
    for part in range(2):
        for grid_row in range(GRID_COLUMNS):
            piece = source[part, :, grid_row * GRID_COLUMNS:(grid_row + 1) * GRID_COLUMNS].astype(F32)
            rows_ref[part, grid_row * 4:grid_row * 4 + 4, :] = piece * sign


def transform(rows_ref, table_ref, bins_ref):
    for sample in range(4):
        volts = jnp.concatenate(
            [rows_ref[part, pl.ds(sample, GRID_COLUMNS, stride=4), :].astype(BF16) for part in range(2)], axis=1
        )
        bins = dot(table_ref[0], volts, (1, 1)) + dot(table_ref[1], volts, (1, 1))
        bins_ref[pl.ds(sample, HALF, stride=8), :] = bins[:HALF]
        bins_ref[pl.ds(sample + 4, HALF, stride=8), :] = bins[HALF:]


def reversal():
    row = lax.broadcasted_iota(jnp.int32, (GRID_COLUMNS, GRID_COLUMNS), 0)
    column = lax.broadcasted_iota(jnp.int32, (GRID_COLUMNS, GRID_COLUMNS), 1)
    return (row + column == GRID_COLUMNS - 1).astype(F32).astype(BF16)


def own_kernel(core_ref, device_ref, own_hbm, table_hbm, pattern_hbm, slots_hbm, inverse_hbm,
               bins_ref, mask_ref, place_ref, table_ref, inverse_ref, scale_ref,
               own_ref, pattern_ref, slots_ref, rows_ref, own_sem, table_sem, pattern_sem, slots_sem, inverse_sem):
    width = GRID_COLUMNS
    slots_copy = pltpu.make_async_copy(slots_hbm, slots_ref, slots_sem)
    own_copy = pltpu.make_async_copy(own_hbm, own_ref, own_sem)
    table_copy = pltpu.make_async_copy(table_hbm, table_ref, table_sem)
    pattern_copy = pltpu.make_async_copy(pattern_hbm, pattern_ref, pattern_sem)
    slots_copy.start()
    own_copy.start()
    pattern_copy.start()
    table_copy.start()
    inverse_copy = pltpu.make_async_copy(inverse_hbm, inverse_ref, inverse_sem)
    inverse_copy.start()
    reverse = reversal()
    slots_copy.wait()
    order = slots_ref[...].astype(F32)
    low, high = order[:, :width], order[:, width:]
    ahead = [pltpu.roll(half, 1, 1) for half in (high, low)]
    behind = [dot(half.astype(BF16), reverse, (1, 0)) for half in (low, high)]
    first = lax.broadcasted_iota(jnp.int32, (1, width), 1) == 0
    lane_slot = jnp.concatenate([jnp.where(first, -1.0, half) for half in ahead + behind], axis=1).astype(jnp.int32)
    index = lax.broadcasted_iota(jnp.int32, (4 * width, 4 * width), 0)
    slot = 2 * (index // 4) + (index // 2) % 2
    mirrored = lax.broadcasted_iota(jnp.int32, (4 * width, 4 * width), 1) >= 2 * width
    weight = jnp.where(mirrored & (index % 2 == 1), -0.5, 0.5)
    place_ref[...] = jnp.where(lane_slot == slot, weight, 0.0).astype(BF16)
    pattern_copy.wait()
    valid = (pattern_ref[...] >= 0).astype(F32).astype(BF16)
    for which in range(2):
        mask_ref[which] = skew(dot(reverse, valid, (1, which)))
    lag = lax.broadcasted_iota(jnp.int32, (1, BINS), 1) - (width - 1)
    reach = width - jnp.abs(lag).astype(F32)
    stack = lax.broadcasted_iota(jnp.int32, (1, BINS), 1)
    for slot in range(2):
        mine = slots_ref[...] == 2 * device_ref[0] + slot
        key = jnp.sum(jnp.where(mine, stack, 0), axis=1, keepdims=True)
        count = jnp.sum((pattern_ref[...] == key).astype(F32), axis=(0, 1), keepdims=True)
        scale_ref[slot:slot + 1, :] = 1.0 / jnp.sqrt(2.0 * TIME_SAMPLES * jnp.maximum(count * reach, 1.0))
    own_copy.wait()
    spread(own_ref, rows_ref, core_ref[0])
    table_copy.wait()
    transform(rows_ref, table_ref, bins_ref)
    inverse_copy.wait()


def stack_kernel(core_ref, peer_ref, own_bins_ref, mask_ref, place_ref, table_ref, out_ref,
                 rows_ref, peer_bins_ref, sums_ref, left_ref, right_ref, gram_ref):
    width = GRID_COLUMNS
    spread(peer_ref, rows_ref, core_ref[0])
    transform(rows_ref, table_ref, peer_bins_ref)
    reverse = reversal()
    minus = jnp.where(lax.broadcasted_iota(jnp.int32, (8, width), 0) < 4, -1.0, 1.0).astype(F32)

    lane = lax.broadcasted_iota(jnp.int32, (8, width), 1)
    sublane = lax.broadcasted_iota(jnp.int32, (8, width), 0)

    def gather_rows(tiles):
        fours = []
        for bin in range(4):
            near, far = tiles[bin], tiles[bin + 4]
            crossed = jnp.where(sublane < 4, far, near)
            fours.append(jnp.where(sublane < 4, near, far) + pltpu.roll(crossed, 4, 0))
        twos = []
        for bin in range(2):
            near, far = fours[bin], fours[bin + 2]
            twos.append(jnp.where(sublane % 4 < 2, near + pltpu.roll(near, 6, 0), far + pltpu.roll(far, 2, 0)))
        near, far = twos
        return jnp.where(sublane % 2 == 0, near + pltpu.roll(near, 7, 0), far + pltpu.roll(far, 1, 0))

    def turn_bins(step):
        lefts = []
        for inner in range(8):
            first = step * 64 + inner * 8
            left, right = [], []
            for source in (own_bins_ref, peer_bins_ref):
                tile = source[first:first + 8, :]
                left.append(tile)
                right.append(tile + minus * pltpu.roll(tile, 4, 0))
            left_high, left_low = halves(jnp.concatenate(left, axis=0))
            right_high, right_low = halves(jnp.concatenate(right, axis=0))
            lefts += [left_high, left_high, left_low, left_low]
            right_ref[step * 8 + inner] = jnp.concatenate([right_high, right_low, right_high, right_low], axis=0)
        left_ref[step] = dot(reverse, jnp.concatenate(lefts, axis=0), (1, 1)).astype(BF16)

    def gram_bins(step):
        for pair in range(4):
            rights = []
            for inner in range(2):
                right = right_ref[step * 8 + pair * 2 + inner]
                empty = jnp.zeros_like(right)
                rights.append(jnp.concatenate([empty, right] if inner else [right, empty], axis=1))
            left = left_ref[step, :, pair * width:(pair + 1) * width]
            gram_ref[step * 4 + pair] = dot(left, jnp.concatenate(rights, axis=0), (1, 0))

    def sum_bins(step):
        totals = [[[None] * 4 for bin in range(8)] for which in range(2)]
        for group in range(0, 8, BATCH):
            for tile in range(16):
                span = slice(tile * 8, tile * 8 + 8)
                below = lane > sublane + tile * 8
                masks = [mask_ref[which, span, :] for which in range(2)]
                for bin in range(group, group + BATCH):
                    lanes = slice(bin % 2 * width, bin % 2 * width + width)
                    shift = (1 + 8 * tile) % width
                    product = gram_ref[step * 4 + bin // 2, span, lanes]
                    product = pltpu.roll(product, shift, 1, stride=1, stride_axis=0)
                    for which in range(2):
                        term = product * masks[which]
                        total, lower = totals[which][bin][:2]
                        total = total + term if tile else term
                        totals[which][bin] = [total, jnp.where(below, total, lower if tile else 0.0)]
        lines = []
        for which in range(2):
            total, lower = [gather_rows([totals[which][bin][kind] for bin in range(8)]) for kind in range(2)]
            lines += [total - lower, lower]
        sums_ref[step * 8:step * 8 + 8, :] = jnp.concatenate(lines, axis=1)

    steps = HALF // 8
    for step in range(steps + 2):
        if step < steps:
            turn_bins(step)
        if 1 <= step <= steps:
            gram_bins(step - 1)
        if 2 <= step:
            sum_bins(step - 2)
    sums_high, sums_low = halves(sums_ref[...])
    out_ref[...] = dot(place_ref[...], sums_high, (1, 1)) + dot(place_ref[...], sums_low, (1, 1))


def owner_kernel(parts_ref, table_ref, scale_ref, out_ref):
    lane = lax.broadcasted_iota(jnp.int32, (1, BINS), 1)
    lines = []
    for core in range(2):
        for chan in range(CHAN):
            total = None
            for near in range(2):
                first = ((chan * 2 + near) * 2 + core) * 16
                part = jnp.sum(parts_ref[first:first + 16], axis=0)
                total = part if total is None else total + part
            for slot in range(2):
                real, imag = total[2 * slot:2 * slot + 1], total[2 * slot + 1:2 * slot + 2]
                lines.append(jnp.concatenate([real, imag], axis=1))
                lines.append(jnp.concatenate([imag, -real], axis=1))
    high, low = halves(jnp.concatenate(lines, axis=0))
    turned = dot(high, table_ref[0], (1, 0)) + dot(low, table_ref[0], (1, 0)) + dot(high, table_ref[1], (1, 0))
    turned = turned[:8] + jnp.where(lane % 2 == 1, 1.0, -1.0) * turned[8:]
    for slot in range(2):
        scale = scale_ref[slot:slot + 1, :]
        for chan in range(CHAN):
            for part in range(2):
                line = chan * 4 + slot * 2 + part
                value = turned[line:line + 1] * scale
                out_ref[slot, 2 * chan + part:2 * chan + part + 1, :] = value[:, :BINS - 1]


def per_device(volts, pattern, owner_slot):
    width = GRID_COLUMNS
    row_index = lax.axis_index("row")
    core = (row_index % 2).reshape(1)
    device = lax.axis_index(("row", "col")).reshape(1)
    row_count = lax.axis_size("row")
    swap = [(i, i ^ 1) for i in range(row_count)]
    peer = lax.ppermute(volts, "row", swap)
    vmem = pl.BlockSpec(memory_space=pltpu.VMEM)
    smem = pl.BlockSpec(memory_space=pltpu.SMEM)
    anywhere = pl.BlockSpec(memory_space=pltpu.HBM)
    operands = (volts, jnp.asarray(forward_table()), pattern, owner_slot[None], jnp.asarray(inverse_table()))
    *prepared, inverse, scale = pl.pallas_call(
        own_kernel,
        out_shape=[
            jax.ShapeDtypeStruct((8 * HALF, width), F32),
            jax.ShapeDtypeStruct((2, width, width), F32),
            jax.ShapeDtypeStruct((4 * width, 4 * width), BF16),
            jax.ShapeDtypeStruct((2, BINS, BINS), BF16),
            jax.ShapeDtypeStruct((2, BINS, BINS), BF16),
            jax.ShapeDtypeStruct((2, BINS), F32),
        ],
        in_specs=[smem] * 2 + [anywhere] * 5,
        out_specs=[vmem] * 6,
        scratch_shapes=[
            pltpu.VMEM(volts.shape, BF16),
            pltpu.VMEM(pattern.shape, jnp.int32),
            pltpu.VMEM((1, 2 * width), jnp.int32),
            pltpu.VMEM((2, 4 * width, width), F32),
            pltpu.SemaphoreType.DMA,
            pltpu.SemaphoreType.DMA,
            pltpu.SemaphoreType.DMA,
            pltpu.SemaphoreType.DMA,
            pltpu.SemaphoreType.DMA,
        ],
        compiler_params=pltpu.CompilerParams(vmem_limit_bytes=16 * 2 ** 20),
        name="own_kernel",
    )(core, device, *[pltpu.with_memory_space_constraint(operand, pltpu.HBM) for operand in operands])
    partial = pl.pallas_call(
        stack_kernel,
        out_shape=jax.ShapeDtypeStruct((4 * width, HALF), F32),
        in_specs=[smem] + [vmem] * 5,
        out_specs=vmem,
        scratch_shapes=[
            pltpu.VMEM((2, 4 * width, width), F32),
            pltpu.VMEM((8 * HALF, width), F32),
            pltpu.VMEM((HALF, 4 * width), F32),
            pltpu.VMEM((HALF // 8, width, 4 * width), BF16),
            pltpu.VMEM((HALF, 64, width), BF16),
            pltpu.VMEM((HALF // 2, width, 2 * width), F32),
        ],
        compiler_params=pltpu.CompilerParams(vmem_limit_bytes=32 * 2 ** 20),
        name="stack_kernel",
    )(core, peer, *prepared)
    parts = lax.all_to_all(partial.reshape(width, 4, HALF), ("row", "col"), split_axis=0, concat_axis=0, tiled=True)
    return pl.pallas_call(
        owner_kernel,
        out_shape=jax.ShapeDtypeStruct((2, 2 * CHAN, BINS - 1), F32),
        in_specs=[vmem] * 3,
        out_specs=vmem,
        compiler_params=pltpu.CompilerParams(vmem_limit_bytes=16 * 2 ** 20),
        name="owner_kernel",
    )(parts, inverse, scale)


def solution(mesh):
    return jax.shard_map(
        per_device,
        mesh=mesh,
        in_specs=(P(None, ("row", "col"), None), P(), P()),
        out_specs=P(("row", "col"), None, None),
        check_vma=False,
    )
```

```python
import jax
import jax.numpy as jnp
import numpy as np
from jax import lax
from jax.experimental import pallas as pl
from jax.experimental.pallas import tpu as pltpu
from jax.sharding import PartitionSpec as P

GRID_COLUMNS = 128
CHAN = 2
CHUNKS = 1
TIME_SAMPLES = 256
BINS = 2 * GRID_COLUMNS
HALF = BINS // 2
F32 = jnp.float32
BF16 = jnp.bfloat16


def split_table(table):
    table = table.astype(np.float32)
    high = table.astype(jnp.bfloat16)
    low = (table - high.astype(np.float32)).astype(jnp.bfloat16)
    return np.stack([high, low])


def forward_table():
    angle = 2.0 * np.pi * np.outer(np.arange(HALF), np.arange(GRID_COLUMNS)) / BINS
    cosine, sine = np.cos(angle), np.sin(angle)
    return np.concatenate(split_table(np.concatenate([cosine, sine], axis=1)))


def inverse_table():
    lag = np.arange(BINS) - (GRID_COLUMNS - 1)
    angle = 2.0 * np.pi * np.outer(np.arange(HALF), lag) / BINS
    return split_table(np.concatenate([np.cos(angle), np.sin(angle)]) / BINS)


def dot(left, right, contract):
    return lax.dot_general(left, right, ((contract[:1], contract[1:]), ((), ())), preferred_element_type=F32)


def halves(value):
    high = value.astype(BF16)
    return high, (value - high.astype(F32)).astype(BF16)


def skew(value):
    return pltpu.roll(value, 1, 1, stride=1, stride_axis=0)


TURN = 4
LAG_TURN = 9
LAG_GRAM = 1


def spread(source, rows_ref, core, grid_rows):
    lane = lax.broadcasted_iota(jnp.int32, (1, GRID_COLUMNS), 1)
    sign = jnp.where((lane % 2 == 1) & (core == 1), -1.0, 1.0).astype(F32)
    for part in range(2):
        for grid_row in grid_rows:
            piece = source[part, :, grid_row * GRID_COLUMNS:(grid_row + 1) * GRID_COLUMNS].astype(F32)
            rows_ref[part, grid_row * 4:grid_row * 4 + 4, :] = piece * sign


def transform(rows_ref, table_ref, bins_ref):
    for sample in range(4):
        real, imag = [rows_ref[part, pl.ds(sample, GRID_COLUMNS, stride=4), :].astype(BF16) for part in range(2)]
        volts = jnp.concatenate([jnp.concatenate([real, imag], axis=1), jnp.concatenate([imag, -real], axis=1)], axis=0)
        bins = dot(table_ref[...], volts, (1, 1))
        bins = bins[:HALF] + bins[HALF:]
        bins_ref[pl.ds(sample, HALF, stride=8), :] = bins[:, :GRID_COLUMNS]
        bins_ref[pl.ds(sample + 4, HALF, stride=8), :] = bins[:, GRID_COLUMNS:]


def reversal():
    row = lax.broadcasted_iota(jnp.int32, (GRID_COLUMNS, GRID_COLUMNS), 0)
    column = lax.broadcasted_iota(jnp.int32, (GRID_COLUMNS, GRID_COLUMNS), 1)
    return (row + column == GRID_COLUMNS - 1).astype(F32).astype(BF16)


def own_kernel(core_ref, device_ref, own_hbm, table_hbm, pattern_hbm, slots_hbm,
               bins_ref, mask_ref, place_ref, table_ref, scale_ref,
               own_ref, pattern_ref, slots_ref, rows_ref, own_sem, table_sem, pattern_sem, slots_sem):
    width = GRID_COLUMNS
    chunk = width // CHUNKS
    table_copy = pltpu.make_async_copy(table_hbm, table_ref, table_sem)
    pattern_copy = pltpu.make_async_copy(pattern_hbm, pattern_ref, pattern_sem)
    slots_copy = pltpu.make_async_copy(slots_hbm, slots_ref, slots_sem)
    slots_copy.start()
    pattern_copy.start()
    own_copies = []
    for index in range(CHUNKS):
        span = (slice(None), slice(None), pl.ds(index * chunk * width, chunk * width))
        own_copies.append(pltpu.make_async_copy(own_hbm.at[span], own_ref.at[span], own_sem.at[index]))
        own_copies[-1].start()
    table_copy.start()
    reverse = reversal()
    slots_copy.wait()
    order = slots_ref[...].astype(F32)
    low, high = order[:, :width], order[:, width:]
    ahead = [pltpu.roll(half, 1, 1) for half in (high, low)]
    behind = [dot(half.astype(BF16), reverse, (1, 0)) for half in (low, high)]
    first = lax.broadcasted_iota(jnp.int32, (1, width), 1) == 0
    lane_slot = jnp.concatenate([jnp.where(first, -1.0, half) for half in ahead + behind], axis=1).astype(jnp.int32)
    index = lax.broadcasted_iota(jnp.int32, (4 * width, 4 * width), 0)
    slot = 2 * (index // 4) + (index // 2) % 2
    mirrored = lax.broadcasted_iota(jnp.int32, (4 * width, 4 * width), 1) >= 2 * width
    weight = jnp.where(mirrored & (index % 2 == 1), -0.5, 0.5)
    place_ref[...] = jnp.where(lane_slot == slot, weight, 0.0).astype(BF16)
    pattern_copy.wait()
    valid = (pattern_ref[...] >= 0).astype(F32).astype(BF16)
    for which in range(2):
        mask_ref[which] = skew(dot(reverse, valid, (1, which)))
    lag = lax.broadcasted_iota(jnp.int32, (1, BINS), 1) - (width - 1)
    reach = width - jnp.abs(lag).astype(F32)
    stack = lax.broadcasted_iota(jnp.int32, (1, BINS), 1)
    for slot in range(2):
        mine = slots_ref[...] == 2 * device_ref[0] + slot
        key = jnp.sum(jnp.where(mine, stack, 0), axis=1, keepdims=True)
        count = jnp.sum((pattern_ref[...] == key).astype(F32), axis=(0, 1), keepdims=True)
        scale_ref[slot:slot + 1, :] = 1.0 / jnp.sqrt(2.0 * TIME_SAMPLES * jnp.maximum(count * reach, 1.0))
    for index in range(CHUNKS):
        own_copies[index].wait()
        spread(own_ref, rows_ref, core_ref[0], range(index * chunk, (index + 1) * chunk))
    table_copy.wait()
    transform(rows_ref, table_ref, bins_ref)


def stack_kernel(core_ref, peer_ref, own_bins_ref, mask_ref, place_ref, table_ref, inverse_hbm, out_ref, inverse_ref,
                 inverse_sem, rows_ref, peer_bins_ref, sums_ref, left_ref, right_ref, gram_ref):
    width = GRID_COLUMNS
    inverse_copy = pltpu.make_async_copy(inverse_hbm, inverse_ref, inverse_sem)
    inverse_copy.start()
    spread(peer_ref, rows_ref, core_ref[0], range(width))
    transform(rows_ref, table_ref, peer_bins_ref)
    reverse = reversal()
    minus = jnp.where(lax.broadcasted_iota(jnp.int32, (8, width), 0) < 4, -1.0, 1.0).astype(F32)

    lane = lax.broadcasted_iota(jnp.int32, (8, width), 1)
    sublane = lax.broadcasted_iota(jnp.int32, (8, width), 0)

    def gather_rows(tiles):
        fours = []
        for bin in range(4):
            near, far = tiles[bin], tiles[bin + 4]
            crossed = jnp.where(sublane < 4, far, near)
            fours.append(jnp.where(sublane < 4, near, far) + pltpu.roll(crossed, 4, 0))
        twos = []
        for bin in range(2):
            near, far = fours[bin], fours[bin + 2]
            twos.append(jnp.where(sublane % 4 < 2, near + pltpu.roll(near, 6, 0), far + pltpu.roll(far, 2, 0)))
        near, far = twos
        return jnp.where(sublane % 2 == 0, near + pltpu.roll(near, 7, 0), far + pltpu.roll(far, 1, 0))

    def turn_pairs(first_pair):
        lefts = []
        for bin in range(first_pair * 2, first_pair * 2 + TURN * 2):
            left, right = [], []
            for source in (own_bins_ref, peer_bins_ref):
                tile = source[bin * 8:bin * 8 + 8, :]
                left.append(tile)
                right.append(tile + minus * pltpu.roll(tile, 4, 0))
            left_high, left_low = halves(jnp.concatenate(left, axis=0))
            right_high, right_low = halves(jnp.concatenate(right, axis=0))
            lefts += [left_high, left_high, left_low, left_low]
            right_ref[bin] = jnp.concatenate([right_high, right_low, right_high, right_low], axis=0)
        turned = dot(reverse, jnp.concatenate(lefts, axis=0), (1, 1)).astype(BF16)
        for pair in range(TURN):
            left_ref[first_pair + pair] = turned[:, pair * width:(pair + 1) * width]

    def gram_pair(pair):
        rights = []
        for inner in range(2):
            right = right_ref[pair * 2 + inner]
            empty = jnp.zeros_like(right)
            rights.append(jnp.concatenate([empty, right] if inner else [right, empty], axis=1))
        left = left_ref[pair]
        gram_ref[pair] = dot(left, jnp.concatenate(rights, axis=0), (1, 0))

    def sum_pair(pair):
        totals = [[[None] * 2 for inner in range(2)] for which in range(2)]
        for tile in range(16):
            span = slice(tile * 8, tile * 8 + 8)
            below = lane > sublane + tile * 8
            for inner in range(2):
                product = gram_ref[pair, span, inner * width:(inner + 1) * width]
                product = pltpu.roll(product, (1 + 8 * tile) % width, 1, stride=1, stride_axis=0)
                for which in range(2):
                    term = product * mask_ref[which, span, :]
                    total, lower = totals[which][inner]
                    total = total + term if tile else term
                    totals[which][inner] = [total, jnp.where(below, total, lower if tile else 0.0)]
        return totals

    pairs = HALF // 2
    held = []
    for pair in range(-LAG_TURN, pairs + LAG_GRAM):
        if (pair + LAG_TURN) % TURN == 0 and pair + LAG_TURN < pairs:
            turn_pairs(pair + LAG_TURN)
        if 0 <= pair < pairs:
            gram_pair(pair)
        if 0 <= pair - LAG_GRAM:
            held.append(sum_pair(pair - LAG_GRAM))
        if len(held) == 4:
            step = (pair - LAG_GRAM) // 4
            lines = []
            for which in range(2):
                total, lower = [
                    gather_rows([held[bin // 2][which][bin % 2][kind] for bin in range(8)]) for kind in range(2)
                ]
                lines += [total - lower, lower]
            sums_ref[step * 8:step * 8 + 8, :] = jnp.concatenate(lines, axis=1)
            held = []
    both = dot(place_ref[...], jnp.concatenate(halves(sums_ref[...]), axis=0), (1, 1))
    out_ref[...] = both[:, :HALF] + both[:, HALF:]
    inverse_copy.wait()


def owner_kernel(parts_ref, table_ref, scale_ref, out_ref):
    lane = lax.broadcasted_iota(jnp.int32, (1, BINS), 1)
    lines = []
    for core in range(2):
        for chan in range(CHAN):
            total = None
            for near in range(2):
                first = ((chan * 2 + near) * 2 + core) * 16
                part = jnp.sum(parts_ref[first:first + 16], axis=0)
                total = part if total is None else total + part
            for slot in range(2):
                real, imag = total[2 * slot:2 * slot + 1], total[2 * slot + 1:2 * slot + 2]
                lines.append(jnp.concatenate([real, imag], axis=1))
                lines.append(jnp.concatenate([imag, -real], axis=1))
    high, low = halves(jnp.concatenate(lines, axis=0))
    turned = dot(high, table_ref[0], (1, 0)) + dot(low, table_ref[0], (1, 0)) + dot(high, table_ref[1], (1, 0))
    turned = turned[:8] + jnp.where(lane % 2 == 1, 1.0, -1.0) * turned[8:]
    for slot in range(2):
        scale = scale_ref[slot:slot + 1, :]
        for chan in range(CHAN):
            for part in range(2):
                line = chan * 4 + slot * 2 + part
                value = turned[line:line + 1] * scale
                out_ref[slot, 2 * chan + part:2 * chan + part + 1, :] = value[:, :BINS - 1]


def per_device(volts, pattern, owner_slot):
    width = GRID_COLUMNS
    row_index = lax.axis_index("row")
    core = (row_index % 2).reshape(1)
    device = lax.axis_index(("row", "col")).reshape(1)
    row_count = lax.axis_size("row")
    swap = [(i, i ^ 1) for i in range(row_count)]
    peer = lax.ppermute(volts, "row", swap)
    vmem = pl.BlockSpec(memory_space=pltpu.VMEM)
    smem = pl.BlockSpec(memory_space=pltpu.SMEM)
    anywhere = pl.BlockSpec(memory_space=pltpu.HBM)
    operands = (volts, jnp.asarray(forward_table()), pattern, owner_slot[None])
    *prepared, scale = pl.pallas_call(
        own_kernel,
        out_shape=[
            jax.ShapeDtypeStruct((8 * HALF, width), F32),
            jax.ShapeDtypeStruct((2, width, width), F32),
            jax.ShapeDtypeStruct((4 * width, 4 * width), BF16),
            jax.ShapeDtypeStruct((BINS, BINS), BF16),
            jax.ShapeDtypeStruct((2, BINS), F32),
        ],
        in_specs=[smem] * 2 + [anywhere] * 4,
        out_specs=[vmem] * 5,
        scratch_shapes=[
            pltpu.VMEM(volts.shape, BF16),
            pltpu.VMEM(pattern.shape, jnp.int32),
            pltpu.VMEM((1, 2 * width), jnp.int32),
            pltpu.VMEM((2, 4 * width, width), F32),
            pltpu.SemaphoreType.DMA((CHUNKS,)),
            pltpu.SemaphoreType.DMA,
            pltpu.SemaphoreType.DMA,
            pltpu.SemaphoreType.DMA,
        ],
        compiler_params=pltpu.CompilerParams(vmem_limit_bytes=16 * 2 ** 20),
        name="own_kernel",
    )(core, device, *[pltpu.with_memory_space_constraint(operand, pltpu.HBM) for operand in operands])
    partial, inverse = pl.pallas_call(
        stack_kernel,
        out_shape=[jax.ShapeDtypeStruct((4 * width, HALF), F32), jax.ShapeDtypeStruct((2, BINS, BINS), BF16)],
        in_specs=[smem] + [vmem] * 5 + [anywhere],
        out_specs=[vmem] * 2,
        scratch_shapes=[
            pltpu.SemaphoreType.DMA,
            pltpu.VMEM((2, 4 * width, width), F32),
            pltpu.VMEM((8 * HALF, width), F32),
            pltpu.VMEM((HALF, 4 * width), F32),
            pltpu.VMEM((HALF // 2, width, width), BF16),
            pltpu.VMEM((HALF, 64, width), BF16),
            pltpu.VMEM((HALF // 2, width, 2 * width), F32),
        ],
        compiler_params=pltpu.CompilerParams(vmem_limit_bytes=32 * 2 ** 20),
        name="stack_kernel",
    )(core, peer, *prepared, pltpu.with_memory_space_constraint(jnp.asarray(inverse_table()), pltpu.HBM))
    parts = lax.all_to_all(partial.reshape(width, 4, HALF), ("row", "col"), split_axis=0, concat_axis=0, tiled=True)
    return pl.pallas_call(
        owner_kernel,
        out_shape=jax.ShapeDtypeStruct((2, 2 * CHAN, BINS - 1), F32),
        in_specs=[vmem] * 3,
        out_specs=vmem,
        compiler_params=pltpu.CompilerParams(vmem_limit_bytes=16 * 2 ** 20),
        name="owner_kernel",
    )(parts, inverse, scale)


def solution(mesh):
    return jax.shard_map(
        per_device,
        mesh=mesh,
        in_specs=(P(None, ("row", "col"), None), P(), P()),
        out_specs=P(("row", "col"), None, None),
        check_vma=False,
    )
```

```python
import jax
import jax.numpy as jnp
import numpy as np
from jax import lax
from jax.experimental import pallas as pl
from jax.experimental.pallas import tpu as pltpu
from jax.sharding import PartitionSpec as P

GRID_COLUMNS = 128
CHAN = 2
TIME_SAMPLES = 256
BINS = 2 * GRID_COLUMNS
HALF = BINS // 2
F32 = jnp.float32
BF16 = jnp.bfloat16


def split_table(table):
    table = table.astype(np.float32)
    high = table.astype(jnp.bfloat16)
    low = (table - high.astype(np.float32)).astype(jnp.bfloat16)
    return np.stack([high, low])


def forward_table():
    angle = 2.0 * np.pi * np.outer(np.arange(HALF), np.arange(GRID_COLUMNS)) / BINS
    cosine, sine = np.cos(angle), np.sin(angle)
    table = np.concatenate([cosine, sine], axis=1)
    tables = [np.concatenate(split_table(table * sign)) for sign in (1.0, np.tile([1.0, -1.0], GRID_COLUMNS))]
    return np.stack(tables)


def inverse_table():
    lag = np.arange(BINS) - (GRID_COLUMNS - 1)
    angle = 2.0 * np.pi * np.outer(np.arange(HALF), lag) / BINS
    return split_table(np.concatenate([np.cos(angle), np.sin(angle)]) / BINS)


def dot(left, right, contract):
    return lax.dot_general(left, right, ((contract[:1], contract[1:]), ((), ())), preferred_element_type=F32)


def halves(value):
    high = value.astype(BF16)
    return high, (value - high.astype(F32)).astype(BF16)


def skew(value):
    return pltpu.roll(value, 1, 1, stride=1, stride_axis=0)


TURN = 2
LAG_TURN = 10
LAG_GRAM = 1


def spread(source, rows_ref):
    for part in range(2):
        for grid_row in range(GRID_COLUMNS):
            piece = source[part, :, grid_row * GRID_COLUMNS:(grid_row + 1) * GRID_COLUMNS]
            rows_ref[part, grid_row * 4:grid_row * 4 + 4, :] = piece.astype(F32)


def transform(rows_ref, table_ref, bins_ref):
    for sample in range(4):
        real, imag = [rows_ref[part, pl.ds(sample, GRID_COLUMNS, stride=4), :].astype(BF16) for part in range(2)]
        volts = jnp.concatenate([jnp.concatenate([real, imag], axis=1), jnp.concatenate([imag, -real], axis=1)], axis=0)
        bins = dot(table_ref[...], volts, (1, 1))
        bins = bins[:HALF] + bins[HALF:]
        bins_ref[pl.ds(sample, HALF, stride=8), :] = bins[:, :GRID_COLUMNS]
        bins_ref[pl.ds(sample + 4, HALF, stride=8), :] = bins[:, GRID_COLUMNS:]


def reversal():
    row = lax.broadcasted_iota(jnp.int32, (GRID_COLUMNS, GRID_COLUMNS), 0)
    column = lax.broadcasted_iota(jnp.int32, (GRID_COLUMNS, GRID_COLUMNS), 1)
    return (row + column == GRID_COLUMNS - 1).astype(F32).astype(BF16)


def own_kernel(core_ref, device_ref, own_hbm, table_hbm, pattern_hbm, slots_hbm,
               bins_ref, mask_ref, place_ref, table_ref, scale_ref,
               own_ref, pattern_ref, slots_ref, rows_ref, own_sem, table_sem, pattern_sem, slots_sem):
    width = GRID_COLUMNS
    table_copy = pltpu.make_async_copy(table_hbm.at[core_ref[0]], table_ref, table_sem)
    pattern_copy = pltpu.make_async_copy(pattern_hbm, pattern_ref, pattern_sem)
    slots_copy = pltpu.make_async_copy(slots_hbm, slots_ref, slots_sem)
    slots_copy.start()
    pattern_copy.start()
    own_copy = pltpu.make_async_copy(own_hbm, own_ref, own_sem)
    own_copy.start()
    table_copy.start()
    reverse = reversal()
    slots_copy.wait()
    order = slots_ref[...].astype(F32)
    low, high = order[:, :width], order[:, width:]
    ahead = [pltpu.roll(half, 1, 1) for half in (high, low)]
    behind = [dot(half.astype(BF16), reverse, (1, 0)) for half in (low, high)]
    first = lax.broadcasted_iota(jnp.int32, (1, width), 1) == 0
    lane_slot = jnp.concatenate([jnp.where(first, -1.0, half) for half in ahead + behind], axis=1).astype(jnp.int32)
    index = lax.broadcasted_iota(jnp.int32, (4 * width, 4 * width), 0)
    slot = 2 * (index // 4) + (index // 2) % 2
    mirrored = lax.broadcasted_iota(jnp.int32, (4 * width, 4 * width), 1) >= 2 * width
    weight = jnp.where(mirrored & (index % 2 == 1), -0.5, 0.5)
    place_ref[...] = jnp.where(lane_slot == slot, weight, 0.0).astype(BF16)
    pattern_copy.wait()
    valid = (pattern_ref[...] >= 0).astype(F32).astype(BF16)
    for which in range(2):
        mask_ref[which] = skew(dot(reverse, valid, (1, which)))
    lag = lax.broadcasted_iota(jnp.int32, (1, BINS), 1) - (width - 1)
    reach = width - jnp.abs(lag).astype(F32)
    stack = lax.broadcasted_iota(jnp.int32, (1, BINS), 1)
    for slot in range(2):
        mine = slots_ref[...] == 2 * device_ref[0] + slot
        key = jnp.sum(jnp.where(mine, stack, 0), axis=1, keepdims=True)
        count = jnp.sum((pattern_ref[...] == key).astype(F32), axis=(0, 1), keepdims=True)
        scale_ref[slot:slot + 1, :] = 1.0 / jnp.sqrt(2.0 * TIME_SAMPLES * jnp.maximum(count * reach, 1.0))
    own_copy.wait()
    spread(own_ref, rows_ref)
    table_copy.wait()
    transform(rows_ref, table_ref, bins_ref)


def stack_kernel(peer_ref, own_bins_ref, mask_ref, place_ref, table_ref, inverse_hbm, out_ref, inverse_ref,
                 inverse_sem, rows_ref, peer_bins_ref, sums_ref, left_ref, right_ref, gram_ref):
    width = GRID_COLUMNS
    inverse_copy = pltpu.make_async_copy(inverse_hbm, inverse_ref, inverse_sem)
    inverse_copy.start()
    spread(peer_ref, rows_ref)
    transform(rows_ref, table_ref, peer_bins_ref)
    reverse = reversal()
    minus = jnp.where(lax.broadcasted_iota(jnp.int32, (8, width), 0) < 4, -1.0, 1.0).astype(F32)

    lane = lax.broadcasted_iota(jnp.int32, (8, width), 1)
    sublane = lax.broadcasted_iota(jnp.int32, (8, width), 0)
    offset = lane - sublane

    def gather_rows(tiles):
        fours = []
        for bin in range(4):
            near, far = tiles[bin], tiles[bin + 4]
            crossed = jnp.where(sublane < 4, far, near)
            fours.append(jnp.where(sublane < 4, near, far) + pltpu.roll(crossed, 4, 0))
        twos = []
        for bin in range(2):
            near, far = fours[bin], fours[bin + 2]
            twos.append(jnp.where(sublane % 4 < 2, near + pltpu.roll(near, 6, 0), far + pltpu.roll(far, 2, 0)))
        near, far = twos
        return jnp.where(sublane % 2 == 0, near + pltpu.roll(near, 7, 0), far + pltpu.roll(far, 1, 0))

    def turn_pairs(first_pair):
        lefts = []
        for bin in range(first_pair * 2, first_pair * 2 + TURN * 2):
            left, right = [], []
            for source in (own_bins_ref, peer_bins_ref):
                tile = source[bin * 8:bin * 8 + 8, :]
                left.append(tile)
                right.append(tile + minus * pltpu.roll(tile, 4, 0))
            left_high, left_low = halves(jnp.concatenate(left, axis=0))
            right_high, right_low = halves(jnp.concatenate(right, axis=0))
            lefts += [left_high, left_high, left_low, left_low]
            right_ref[bin] = jnp.concatenate([right_high, right_low, right_high, right_low], axis=0)
        turned = dot(reverse, jnp.concatenate(lefts, axis=0), (1, 1)).astype(BF16)
        for pair in range(TURN):
            left_ref[first_pair + pair] = turned[:, pair * width:(pair + 1) * width]

    def gram_pair(pair):
        rights = []
        for inner in range(2):
            right = right_ref[pair * 2 + inner]
            empty = jnp.zeros_like(right)
            rights.append(jnp.concatenate([empty, right] if inner else [right, empty], axis=1))
        left = left_ref[pair]
        gram_ref[pair] = dot(left, jnp.concatenate(rights, axis=0), (1, 0))

    def sum_pair(pair):
        totals = [[[None] * 2 for inner in range(2)] for which in range(2)]
        for tile in range(16):
            span = slice(tile * 8, tile * 8 + 8)
            below = offset > tile * 8
            for inner in range(2):
                product = gram_ref[pair, span, inner * width:(inner + 1) * width]
                product = pltpu.roll(product, (1 + 8 * tile) % width, 1, stride=1, stride_axis=0)
                for which in range(2):
                    term = product * mask_ref[which, span, :]
                    total, lower = totals[which][inner]
                    total = total + term if tile else term
                    totals[which][inner] = [total, jnp.where(below, total, lower if tile else 0.0)]
        return totals

    pairs = HALF // 2
    held = []
    for pair in range(-LAG_TURN, pairs + LAG_GRAM):
        if (pair + LAG_TURN) % TURN == 0 and pair + LAG_TURN < pairs:
            turn_pairs(pair + LAG_TURN)
        if 0 <= pair < pairs:
            gram_pair(pair)
        if 0 <= pair - LAG_GRAM:
            held.append(sum_pair(pair - LAG_GRAM))
        if len(held) == 4:
            step = (pair - LAG_GRAM) // 4
            lines = []
            for which in range(2):
                total, lower = [
                    gather_rows([held[bin // 2][which][bin % 2][kind] for bin in range(8)]) for kind in range(2)
                ]
                lines += [total - lower, lower]
            sums_ref[step * 8:step * 8 + 8, :] = jnp.concatenate(lines, axis=1)
            held = []
    both = dot(place_ref[...], jnp.concatenate(halves(sums_ref[...]), axis=0), (1, 1))
    out_ref[...] = both[:, :HALF] + both[:, HALF:]
    inverse_copy.wait()


def owner_kernel(parts_ref, table_ref, scale_ref, out_ref):
    lane = lax.broadcasted_iota(jnp.int32, (1, BINS), 1)
    lines = []
    for core in range(2):
        for chan in range(CHAN):
            total = None
            for near in range(2):
                first = ((chan * 2 + near) * 2 + core) * 16
                part = jnp.sum(parts_ref[first:first + 16], axis=0)
                total = part if total is None else total + part
            for slot in range(2):
                real, imag = total[2 * slot:2 * slot + 1], total[2 * slot + 1:2 * slot + 2]
                lines.append(jnp.concatenate([real, imag], axis=1))
                lines.append(jnp.concatenate([imag, -real], axis=1))
    high, low = halves(jnp.concatenate(lines, axis=0))
    turned = dot(high, table_ref[0], (1, 0)) + dot(low, table_ref[0], (1, 0)) + dot(high, table_ref[1], (1, 0))
    turned = turned[:8] + jnp.where(lane % 2 == 1, 1.0, -1.0) * turned[8:]
    for slot in range(2):
        scale = scale_ref[slot:slot + 1, :]
        for chan in range(CHAN):
            for part in range(2):
                line = chan * 4 + slot * 2 + part
                value = turned[line:line + 1] * scale
                out_ref[slot, 2 * chan + part:2 * chan + part + 1, :] = value[:, :BINS - 1]


def per_device(volts, pattern, owner_slot):
    width = GRID_COLUMNS
    row_index = lax.axis_index("row")
    core = (row_index % 2).reshape(1)
    device = lax.axis_index(("row", "col")).reshape(1)
    row_count = lax.axis_size("row")
    swap = [(i, i ^ 1) for i in range(row_count)]
    peer = lax.ppermute(volts, "row", swap)
    vmem = pl.BlockSpec(memory_space=pltpu.VMEM)
    smem = pl.BlockSpec(memory_space=pltpu.SMEM)
    anywhere = pl.BlockSpec(memory_space=pltpu.HBM)
    operands = (volts, jnp.asarray(forward_table()), pattern, owner_slot[None])
    *prepared, scale = pl.pallas_call(
        own_kernel,
        out_shape=[
            jax.ShapeDtypeStruct((8 * HALF, width), F32),
            jax.ShapeDtypeStruct((2, width, width), F32),
            jax.ShapeDtypeStruct((4 * width, 4 * width), BF16),
            jax.ShapeDtypeStruct((BINS, BINS), BF16),
            jax.ShapeDtypeStruct((2, BINS), F32),
        ],
        in_specs=[smem] * 2 + [anywhere] * 4,
        out_specs=[vmem] * 5,
        scratch_shapes=[
            pltpu.VMEM(volts.shape, BF16),
            pltpu.VMEM(pattern.shape, jnp.int32),
            pltpu.VMEM((1, 2 * width), jnp.int32),
            pltpu.VMEM((2, 4 * width, width), F32),
            pltpu.SemaphoreType.DMA,
            pltpu.SemaphoreType.DMA,
            pltpu.SemaphoreType.DMA,
            pltpu.SemaphoreType.DMA,
        ],
        compiler_params=pltpu.CompilerParams(vmem_limit_bytes=16 * 2 ** 20),
        name="own_kernel",
    )(core, device, *[pltpu.with_memory_space_constraint(operand, pltpu.HBM) for operand in operands])
    partial, inverse = pl.pallas_call(
        stack_kernel,
        out_shape=[jax.ShapeDtypeStruct((4 * width, HALF), F32), jax.ShapeDtypeStruct((2, BINS, BINS), BF16)],
        in_specs=[vmem] * 5 + [anywhere],
        out_specs=[vmem] * 2,
        scratch_shapes=[
            pltpu.SemaphoreType.DMA,
            pltpu.VMEM((2, 4 * width, width), F32),
            pltpu.VMEM((8 * HALF, width), F32),
            pltpu.VMEM((HALF, 4 * width), F32),
            pltpu.VMEM((HALF // 2, width, width), BF16),
            pltpu.VMEM((HALF, 64, width), BF16),
            pltpu.VMEM((HALF // 2, width, 2 * width), F32),
        ],
        compiler_params=pltpu.CompilerParams(vmem_limit_bytes=32 * 2 ** 20),
        name="stack_kernel",
    )(peer, *prepared, pltpu.with_memory_space_constraint(jnp.asarray(inverse_table()), pltpu.HBM))
    parts = lax.all_to_all(partial.reshape(width, 4, HALF), ("row", "col"), split_axis=0, concat_axis=0, tiled=True)
    return pl.pallas_call(
        owner_kernel,
        out_shape=jax.ShapeDtypeStruct((2, 2 * CHAN, BINS - 1), F32),
        in_specs=[vmem] * 3,
        out_specs=vmem,
        compiler_params=pltpu.CompilerParams(vmem_limit_bytes=16 * 2 ** 20),
        name="owner_kernel",
    )(parts, inverse, scale)


def solution(mesh):
    return jax.shard_map(
        per_device,
        mesh=mesh,
        in_specs=(P(None, ("row", "col"), None), P(), P()),
        out_specs=P(("row", "col"), None, None),
        check_vma=False,
    )
```
